32 devices in a mesh: dp: 8 (over y, x, core), tensor: 4 (over z).
Axes of the slice: x: 2, y: 2, z: 4, core: 2. Of those that a mesh axis runs over, the one named last changes fastest.
Arguments:
- hidden: bfloat16 [4096, 8192], P(('dp', 'tensor')), may hold values from -50 to 50
- out_weight: bfloat16 [128256, 8192], P(('dp', 'tensor')), may hold values from -1 to 1
- loss_mask: int32 [4096], P(('dp', 'tensor')), may hold values from 0 to 1, as said below
- targets: int32 [4096], P(('dp', 'tensor')), may hold values from 0 to 128255
- kept_count: int32 [32], P(('dp', 'tensor')), may hold values from 0 to 1, as said below
Outputs:
- hidden_grad: bfloat16 [4096, 8192], P(('dp', 'tensor'))
- row_loss: float32 [4096], P(('dp', 'tensor'))
The draws below stay inside these ranges and needn't reach their ends.
Inputs may be any that keep to these rules, and one draw needn't show every extreme that they name: `loss_mask`: each device's 128 rows hold at least 1 ones. `kept_count`: some entry equals 1 and some entry equals 0.
All inputs are finite; a program needn't handle non-finite values.
Results may differ from the reference program's by a relative error of at most 0.0026.
Values may be sent and summed in bfloat16 or wider, within the bound.
A program may use at most 128 MiB of HBM per device.

```python
import math
import jax
import jax.numpy as jnp
import numpy as np
from jax import lax

D = 8192
VOCAB = 128256
TOK_DEV = 128
CAP = 1
ROWS = 4096


def weight_rows(key, row_ids):
    base_key = jax.random.fold_in(key, 7)

    def single(vocab_id):
        return jax.random.truncated_normal(jax.random.fold_in(base_key, vocab_id), -6.0, 6.0, (D,), jnp.float32)
    return jax.vmap(single)(row_ids) * D ** (-0.5)


def draw_out_weight(key, part):
    blocks = jnp.arange(VOCAB, dtype=jnp.int32).reshape(256, VOCAB // 256)

    def one_block(block):
        return weight_rows(key, block).astype(jnp.bfloat16)
    values = lax.map(one_block, blocks)
    return values.reshape(VOCAB, D)


def draw_hidden(key, part):
    hidden_key = jax.random.fold_in(key, 3)
    drawn = jax.random.truncated_normal(jax.random.fold_in(hidden_key, 1), -6.0, 6.0, (ROWS, D), jnp.float32)
    return drawn.astype(jnp.bfloat16)


def draw_loss_mask(key, part):
    mask_key = jax.random.fold_in(key, 5)
    devices = ROWS // TOK_DEV
    random_bits = jax.random.randint(jax.random.fold_in(mask_key, 1), (devices, TOK_DEV), 0, 2)

    def one_order(sub_key):
        return jax.random.permutation(sub_key, TOK_DEV)
    orders = jax.vmap(one_order)(jax.random.split(jax.random.fold_in(mask_key, 2), devices))
    positions = jnp.arange(TOK_DEV, dtype=jnp.int32)
    forced = jnp.any(orders[:, :CAP, None] == positions[None, None, :], axis=1)
    return jnp.maximum(random_bits, forced.astype(jnp.int32)).reshape(ROWS).astype(jnp.int32)


def draw_kept_count(key, part):
    count_key = jax.random.fold_in(key, 9)
    devices = ROWS // TOK_DEV
    counts = jax.random.randint(jax.random.fold_in(count_key, 1), (devices,), 0, CAP + 1)
    full_at = jax.random.randint(jax.random.fold_in(count_key, 2), (), 0, devices)
    empty_at = (full_at + jax.random.randint(jax.random.fold_in(count_key, 3), (), 1, devices)) % devices
    device_ids = jnp.arange(devices)
    counts = jnp.where(device_ids == empty_at, 0, counts)
    return jnp.where(device_ids == full_at, CAP, counts).astype(jnp.int32)


def place_ends(result, stream_key, low, top_value):
    shape = result.shape
    place = [jax.random.randint(jax.random.fold_in(stream_key, axis), (), 0, shape[axis]) for axis in range(len(shape))]
    result = result.at[tuple(place)].set(low)
    longest = shape.index(max(shape))
    place[longest] = (place[longest] + 1) % shape[longest]
    return result.at[tuple(place)].set(top_value)


def ranked_wide(key, shape, count, skew):
    weights = [min(1 << octave, count + 1 - (1 << octave)) * (1 << 20) // math.isqrt((1 << octave) ** skew) + 1 for octave in range((count + 1).bit_length()) if 1 << octave <= count]
    width = 1 + sum(weights) // (1 << 30)
    listing = np.cumsum(np.array([max(1, weight // width) for weight in weights]))
    pick = jax.random.randint(jax.random.fold_in(key, 1), shape, 0, int(listing[len(weights) - 1]))
    start = jnp.left_shift(1, jnp.searchsorted(jnp.asarray(listing, jnp.int32), pick, side="right").astype(jnp.int32))
    rank = start - 1 + jax.random.randint(jax.random.fold_in(key, 4), shape, 0, 1 << 30) % jnp.minimum(start, count + 1 - start)
    return jax.random.permutation(jax.random.fold_in(key, 2), count)[rank].astype(jnp.int32)


def setup_inputs(seed: int = 0) -> dict:
    key_list = jax.random.split(jax.random.key(seed), 6)
    hidden = draw_hidden(jax.random.fold_in(key_list[5], 71), 0)
    out_weight = draw_out_weight(jax.random.fold_in(key_list[5], 71), 0)
    loss_mask = draw_loss_mask(jax.random.fold_in(key_list[5], 71), 0)
    targets = place_ends(ranked_wide(key_list[3], (ROWS,), VOCAB, 2), jax.random.fold_in(key_list[3], 3), 0, VOCAB - 1).astype(jnp.int32)
    kept_count = draw_kept_count(jax.random.fold_in(key_list[5], 71), 0)
    return {"hidden": hidden, "out_weight": out_weight, "loss_mask": loss_mask, "targets": targets, "kept_count": kept_count}


loss_scale = 128.0


def reference(hidden, out_weight, loss_mask, targets, kept_count):
    devices = kept_count.shape[0]
    per_device = hidden.shape[0] // devices
    mask_rows = loss_mask.reshape(devices, per_device)
    order_pos = jnp.cumsum(mask_rows, axis=1).astype(jnp.int32) - 1
    kept_row = (mask_rows == 1) & (order_pos < kept_count[:, None])
    slot_ids = jnp.arange(CAP, dtype=jnp.int32)
    slot_hits = kept_row[:, None, :] & (order_pos[:, None, :] == slot_ids[None, :, None])
    positions = jnp.arange(per_device, dtype=jnp.int32)
    local_row = jnp.sum(jnp.where(slot_hits, positions[None, None, :], 0), axis=2).astype(jnp.int32)
    filled = jnp.any(slot_hits, axis=2).reshape(-1)
    offsets = (jnp.arange(devices, dtype=jnp.int32) * per_device)[:, None]
    global_row = (local_row + offsets).reshape(-1).astype(jnp.int32)
    packed = jnp.where(filled[:, None], hidden[global_row], jnp.zeros((), hidden.dtype))
    packed_target = jnp.where(filled, targets[global_row], -1).astype(jnp.int32)
    logits = jnp.dot(packed, out_weight.T, preferred_element_type=jnp.float32)
    row_top = jnp.max(logits, axis=1)
    row_total = jnp.sum(jnp.exp(logits - row_top[:, None]), axis=1)
    log_total = row_top + jnp.log(row_total)
    vocab_ids = jnp.arange(logits.shape[1], dtype=jnp.int32)
    target_hit = vocab_ids[None, :] == packed_target[:, None]
    picked = jnp.sum(jnp.where(target_hit, logits, 0.0), axis=1)
    slot_loss = jnp.where(filled, log_total - picked, 0.0)
    probabilities = jnp.exp(logits - log_total[:, None])
    coefficient = jnp.where(filled[:, None], probabilities - target_hit.astype(logits.dtype), 0.0).astype(jnp.bfloat16)
    slot_grad = jnp.dot(coefficient, out_weight, preferred_element_type=jnp.float32) * loss_scale
    hidden_grad = jnp.zeros((hidden.shape[0], hidden.shape[1]), slot_grad.dtype).at[global_row].add(slot_grad)
    row_loss = jnp.zeros((hidden.shape[0],), slot_loss.dtype).at[global_row].add(slot_loss)
    return hidden_grad.astype(jnp.bfloat16), row_loss
```

```python
import functools

import jax
import jax.numpy as jnp
from jax import lax
from jax.experimental import pallas as pl
from jax.experimental.pallas import tpu as pltpu
from jax.sharding import PartitionSpec as P

CAP = 1


loss_scale = 128.0

CORES = 2
PIECES = 16
TILE = 256
RING = 10
LOW = -1e30


def kernel(
    sizes, kept_ref, mask_ref, target_ref, hidden_ref, weight_ref,
    grad_ref, loss_ref, pos_ref,
    rows, ring, gathered, wide, packed, acc, hit_acc,
    sums, hits, stats,
    core_sums, core_hits, core_stats,
    group_out, group_in, group_stats,
    column_out, column_in, column_stats, column_own,
    rows_sem, ring_sem, send_sem, recv_sem,
):
    chips, depth, vocab_rows, width = sizes
    half = chips * depth
    slots = CORES * half
    piece = width // PIECES
    tiles = -(-vocab_rows // TILE)
    tail = vocab_rows - (tiles - 1) * TILE
    f32, bf16 = jnp.float32, jnp.bfloat16

    dp = lax.axis_index("dp")
    z = lax.axis_index("tensor")
    chip = dp // CORES
    core = dp % CORES
    slot = core * half + chip * depth + z

    def tile_copy(j):
        at = lax.rem(j, RING)
        first = pl.multiple_of((j - 1) * TILE, TILE)
        return pltpu.make_async_copy(
            weight_ref.at[pl.ds(first, TILE)], ring.at[at], ring_sem.at[at]
        )

    tail_copy = pltpu.make_async_copy(
        weight_ref.at[pl.ds((tiles - 1) * TILE, tail)],
        ring.at[0, pl.ds(0, tail)],
        ring_sem.at[0],
    )
    rows_copy = pltpu.make_async_copy(hidden_ref, rows, rows_sem)
    rows_copy.start()
    if tail < TILE:
        zero_from = tail // 16 * 16
        ring[0, zero_from:, :] = jnp.zeros((TILE - zero_from, width), bf16)
    tail_copy.start()
    for j in range(1, min(RING, tiles)):
        tile_copy(j).start()

    chip_peers = [lax.rem(chip + k, chips) for k in range(1, chips)]
    chip_froms = [lax.rem(chip + chips - k, chips) for k in range(1, chips)]
    depth_peers = [lax.rem(z + k, depth) for k in range(1, depth)]
    depth_froms = [lax.rem(z + depth - k, depth) for k in range(1, depth)]
    other = 1 - core

    def to_depth(peer):
        return (dp, peer)

    def to_chip(peer):
        return (peer * CORES + core, z)

    to_core = (chip * CORES + other, z)
    everyone = [to_depth(p) for p in depth_peers] + [to_chip(p) for p in chip_peers] + [to_core]
    barrier = pltpu.get_barrier_semaphore()
    for peer in everyone:
        pl.semaphore_signal(barrier, inc=1, device_id=peer, device_id_type=pl.DeviceIdType.MESH)

    mask = mask_ref[...]
    lanes = lax.broadcasted_iota(jnp.int32, mask.shape, 1)
    count = mask.shape[1]
    kept = kept_ref[0]
    first = jnp.min(jnp.where(mask == 1, lanes, count), axis=1, keepdims=True)
    first = jnp.where(kept > 0, first, count)
    hit = lanes == first
    filled = first < count
    target = jnp.sum(jnp.where(hit, target_ref[...], 0), axis=1, keepdims=True)
    digits = (
        jnp.where(filled, target & 255, -1),
        jnp.where(filled, (target >> 8) & 255, 0),
        jnp.where(filled, target >> 16, 0),
    )
    piece_row = lax.broadcasted_iota(jnp.int32, (PIECES, 128), 0)
    coded = jnp.zeros((PIECES, 128), jnp.int32)
    for k, digit in enumerate(digits):
        coded = jnp.where(piece_row == k, digit, coded)
    own_rows = pl.ds(pl.multiple_of(slot * PIECES, PIECES), PIECES)
    gathered[own_rows, piece:] = coded.astype(f32).astype(bf16)
    select_row = lax.broadcasted_iota(jnp.int32, (PIECES, count), 0)
    hit_rows = jnp.broadcast_to(hit.astype(f32), (PIECES, count))
    rows_copy.wait()
    own = jnp.zeros((PIECES, piece), f32)
    for a in range(PIECES):
        chosen = jnp.where(select_row == a, hit_rows, 0.0).astype(bf16)
        own += jnp.dot(chosen, rows[:, a * piece:(a + 1) * piece], preferred_element_type=f32)
    gathered[own_rows, :piece] = own.astype(bf16)

    started = []
    next_sem = [0]

    def send(src, dst, peer):
        k = next_sem[0]
        next_sem[0] += 1
        copy = pltpu.make_async_remote_copy(
            src_ref=src, dst_ref=dst, send_sem=send_sem.at[k], recv_sem=recv_sem.at[k],
            device_id=peer, device_id_type=pl.DeviceIdType.MESH,
        )
        copy.start()
        started.append(copy)
        return copy

    pl.semaphore_wait(barrier, len(everyone))
    part = gathered.at[own_rows]
    for copy in [send(part, part, to_depth(p)) for p in depth_peers]:
        copy.wait_recv()
    first_row = pl.multiple_of((core * half + chip * depth) * PIECES, PIECES)
    part = gathered.at[pl.ds(first_row, depth * PIECES)]
    for copy in [send(part, part, to_chip(p)) for p in chip_peers]:
        copy.wait_recv()
    first_row = pl.multiple_of(core * (half * PIECES), PIECES)
    part = gathered.at[pl.ds(first_row, half * PIECES)]
    send(part, part, to_core).wait_recv()

    lane_blocks = piece // 128
    for b in range(lane_blocks + 1):
        wide[b] = gathered[:, b * 128:(b + 1) * 128].astype(f32)
    for a in range(PIECES):
        for b in range(lane_blocks):
            low = a * piece + b * 128
            packed[:, low:low + 128] = wide[b, pl.ds(a, slots, stride=PIECES), :].astype(bf16)
    code = [wide[lane_blocks, pl.ds(k, slots, stride=PIECES), :] for k in range(3)]
    slot_target = (code[0] + 256.0 * code[1] + 65536.0 * code[2]).astype(jnp.int32)[:, :1]
    acc[...] = jnp.zeros_like(acc)
    hit_acc[...] = jnp.zeros_like(hit_acc)

    vocab_first = (dp * depth + z) * vocab_rows
    columns = lax.broadcasted_iota(jnp.int32, (slots, TILE), 1)

    def logits_of(at):
        return lax.dot_general(
            packed[...], ring[at], (((1,), (1,)), ((), ())), preferred_element_type=f32
        )

    def absorb(j, logits, top, total, picked):
        at = lax.rem(j, RING)
        begin = jnp.where(j == 0, tiles - 1, j - 1) * TILE
        size = jnp.where(j == 0, tail, TILE)
        valid = columns < size
        logits = jnp.where(valid, logits, LOW)
        here = valid & (columns + (vocab_first + begin) == slot_target)
        later_top = jnp.maximum(top, jnp.max(logits, axis=1, keepdims=True))
        fade = jnp.exp(top - later_top)
        weights = jnp.exp(logits - later_top)
        total = total * fade + jnp.sum(weights, axis=1, keepdims=True)
        picked = picked + jnp.sum(jnp.where(here, logits, 0.0), axis=1, keepdims=True)
        both = jnp.concatenate(
            [jnp.where(here, 0.0, weights), here.astype(f32)], axis=0
        ).astype(bf16)
        for a in range(PIECES):
            cut = slice(a * piece, (a + 1) * piece)
            term = jnp.dot(both, ring[at, :, cut], preferred_element_type=f32)
            acc[:, cut] = acc[:, cut] * fade + term[:slots]
            hit_acc[:, cut] += term[slots:]
        return later_top, total, picked

    def step(j, carry):
        logits, top, total, picked = carry
        tile_copy(j + 1).wait()
        later = logits_of(lax.rem(j + 1, RING))
        top, total, picked = absorb(j, logits, top, total, picked)

        @pl.when(j + RING < tiles)
        def _():
            tile_copy(j + RING).start()

        return later, top, total, picked

    tail_copy.wait()
    start = jnp.zeros((slots, 1), f32)
    carry = (logits_of(0), start + LOW, start, start)
    carry = lax.fori_loop(0, tiles - 1, step, carry)
    top, total, picked = absorb(jnp.int32(tiles - 1), *carry)

    def by_slot(source):
        for a in range(PIECES):
            for b in range(lane_blocks):
                low = a * piece + b * 128
                wide[b, pl.ds(a, slots, stride=PIECES), :] = source[:, low:low + 128]

    by_slot(acc)
    for b in range(lane_blocks):
        sums[:, b * 128:(b + 1) * 128] = wide[b]
    by_slot(hit_acc)
    for b in range(lane_blocks):
        hits[:, b * 128:(b + 1) * 128] = wide[b].astype(bf16)
    stats[...] = jnp.zeros_like(stats)
    for k, value in enumerate((top, total, picked)):
        stats[pl.ds(k, slots, stride=8), :] = jnp.broadcast_to(value, (slots, 128))

    def merge(parts):
        tops = [s[0:1] for _, _, s in parts]
        top = functools.reduce(jnp.maximum, tops)
        fades = [jnp.exp(t - top) for t in tops]
        total = sum(f * s[1:2] for f, (_, _, s) in zip(fades, parts))
        picked = sum(s[2:3] for _, _, s in parts)
        grad = sum(
            jnp.concatenate([f] * lane_blocks, axis=1) * g for f, (g, _, _) in zip(fades, parts)
        )
        target_row = sum(h for _, h, _ in parts)
        return grad, target_row, top, total, picked

    def block_of(top, total, picked):
        row = lax.broadcasted_iota(jnp.int32, (8, 128), 0)
        zero = jnp.zeros((8, 128), f32)
        return jnp.where(row == 0, top, jnp.where(row == 1, total, jnp.where(row == 2, picked, zero)))

    theirs = pl.multiple_of(other * (half * PIECES), PIECES)
    their_stats = pl.multiple_of(other * (half * 8), 8)
    copies = [
        send(stats.at[pl.ds(their_stats, half * 8)], core_stats, to_core),
        send(sums.at[pl.ds(theirs, half * PIECES)], core_sums, to_core),
        send(hits.at[pl.ds(theirs, half * PIECES)], core_hits, to_core),
    ]
    for copy in copies:
        copy.wait_recv()
    mine = pl.multiple_of(core * (half * PIECES), PIECES)
    mine_stats = pl.multiple_of(core * (half * 8), 8)

    def core_merge(s, _):
        at = pl.ds(pl.multiple_of(mine + s * PIECES, PIECES), PIECES)
        at_stats = pl.ds(pl.multiple_of(mine_stats + s * 8, 8), 8)
        there = pl.ds(pl.multiple_of(s * PIECES, PIECES), PIECES)
        there_stats = pl.ds(pl.multiple_of(s * 8, 8), 8)
        grad, target_row, *rest = merge([
            (sums[at], hits[at].astype(f32), stats[at_stats]),
            (core_sums[there], core_hits[there].astype(f32), core_stats[there_stats]),
        ])
        core_sums[there] = grad
        core_stats[there_stats] = block_of(*rest)
        lower = pl.multiple_of(s * (2 * PIECES), PIECES)
        group_out[pl.ds(lower, PIECES)] = grad.astype(bf16)
        group_out[pl.ds(lower + PIECES, PIECES)] = target_row.astype(bf16)
        return 0

    lax.fori_loop(0, half, core_merge, 0, unroll=4)

    span = depth * 2 * PIECES
    copies = []
    for k, peer in enumerate(chip_peers):
        copies.append(send(
            core_stats.at[pl.ds(pl.multiple_of(peer * (depth * 8), 8), depth * 8)],
            group_stats.at[k], to_chip(peer),
        ))
        copies.append(send(
            group_out.at[pl.ds(pl.multiple_of(peer * span, PIECES), span)],
            group_in.at[k], to_chip(peer),
        ))
    for copy in copies:
        copy.wait_recv()
    for s in range(depth):
        at = pl.ds(pl.multiple_of((chip * depth + s) * PIECES, PIECES), PIECES)
        at_stats = pl.ds(pl.multiple_of((chip * depth + s) * 8, 8), 8)
        own_hit = pl.ds(pl.multiple_of((chip * depth + s) * (2 * PIECES) + PIECES, PIECES), PIECES)
        low = s * 2 * PIECES
        parts = [(core_sums[at], group_out[own_hit].astype(f32), core_stats[at_stats])]
        for k in range(chips - 1):
            parts.append((
                group_in[k, low:low + PIECES].astype(f32),
                group_in[k, low + PIECES:low + 2 * PIECES].astype(f32),
                group_stats[k, s * 8:s * 8 + 8],
            ))
        grad, target_row, *rest = merge(parts)
        core_sums[at] = grad
        column_own[s * 8:s * 8 + 8] = block_of(*rest)
        column_out[low:low + PIECES] = grad.astype(bf16)
        column_out[low + PIECES:low + 2 * PIECES] = target_row.astype(bf16)

    copies = []
    for k, peer in enumerate(depth_peers):
        copies.append(send(
            column_own.at[pl.ds(pl.multiple_of(peer * 8, 8), 8)], column_stats.at[k], to_depth(peer)
        ))
        copies.append(send(
            column_out.at[pl.ds(pl.multiple_of(peer * (2 * PIECES), PIECES), 2 * PIECES)],
            column_in.at[k], to_depth(peer),
        ))
    for copy in copies:
        copy.wait_recv()
    parts = [(
        core_sums[pl.ds(pl.multiple_of((chip * depth + z) * PIECES, PIECES), PIECES)],
        column_out[pl.ds(pl.multiple_of(z * (2 * PIECES) + PIECES, PIECES), PIECES)].astype(f32),
        column_own[pl.ds(pl.multiple_of(z * 8, 8), 8)],
    )]
    for k in range(depth - 1):
        parts.append((
            column_in[k, :PIECES].astype(f32), column_in[k, PIECES:].astype(f32), column_stats[k]
        ))
    grad, target_row, top, total, picked = merge(parts)
    log_total = top + jnp.log(total)
    share = jnp.concatenate([1.0 / total] * lane_blocks, axis=1)
    at_target = (jnp.exp(picked - log_total) - 1.0).astype(bf16).astype(f32)
    at_target = jnp.concatenate([at_target] * lane_blocks, axis=1)
    grad = (grad * share + target_row * at_target) * loss_scale
    for a in range(PIECES):
        grad_ref[:, a * piece:(a + 1) * piece] = grad[a:a + 1]
    loss_ref[...] = jnp.where(hit, (log_total - picked)[:, :1], 0.0)
    pos_ref[...] = jnp.broadcast_to(first, pos_ref.shape)
    for copy in started:
        copy.wait_send()


def fused_shards(hidden, out_weight, loss_mask, targets, kept_count):
    count, width = hidden.shape
    vocab_rows = out_weight.shape[0]
    chips = lax.axis_size("dp") // CORES
    depth = lax.axis_size("tensor")
    half = chips * depth
    slots = CORES * half
    piece = width // PIECES
    f32, bf16 = jnp.float32, jnp.bfloat16
    copies = 2 * (depth - 1) + 2 * (chips - 1) + (chips - 1) + (depth - 1) + 4
    vmem, any_space = pl.BlockSpec(memory_space=pltpu.VMEM), pl.BlockSpec(memory_space=pl.ANY)
    row_grad, row_loss, pos = pl.pallas_call(
        functools.partial(kernel, (chips, depth, vocab_rows, width)),
        out_shape=(
            jax.ShapeDtypeStruct((1, width), f32),
            jax.ShapeDtypeStruct((1, count), f32),
            jax.ShapeDtypeStruct((1, count), jnp.int32),
        ),
        in_specs=[pl.BlockSpec(memory_space=pltpu.SMEM), vmem, vmem, any_space, any_space],
        out_specs=(vmem, vmem, vmem),
        scratch_shapes=[
            pltpu.VMEM((count, width), bf16),
            pltpu.VMEM((RING, TILE, width), bf16),
            pltpu.VMEM((slots * PIECES, piece + 128), bf16),
            pltpu.VMEM((piece // 128 + 1, slots * PIECES, 128), f32),
            pltpu.VMEM((slots, width), bf16),
            pltpu.VMEM((slots, width), f32),
            pltpu.VMEM((slots, width), f32),
            pltpu.VMEM((slots * PIECES, piece), f32),
            pltpu.VMEM((slots * PIECES, piece), bf16),
            pltpu.VMEM((slots * 8, 128), f32),
            pltpu.VMEM((half * PIECES, piece), f32),
            pltpu.VMEM((half * PIECES, piece), bf16),
            pltpu.VMEM((half * 8, 128), f32),
            pltpu.VMEM((half * 2 * PIECES, piece), bf16),
            pltpu.VMEM((chips - 1, depth * 2 * PIECES, piece), bf16),
            pltpu.VMEM((chips - 1, depth * 8, 128), f32),
            pltpu.VMEM((depth * 2 * PIECES, piece), bf16),
            pltpu.VMEM((depth - 1, 2 * PIECES, piece), bf16),
            pltpu.VMEM((depth - 1, 8, 128), f32),
            pltpu.VMEM((depth * 8, 128), f32),
            pltpu.SemaphoreType.DMA,
            pltpu.SemaphoreType.DMA((RING,)),
            pltpu.SemaphoreType.DMA((copies,)),
            pltpu.SemaphoreType.DMA((copies,)),
        ],
        compiler_params=pltpu.CompilerParams(
            collective_id=0, has_side_effects=True, vmem_limit_bytes=60 * 2**20
        ),
        cost_estimate=pl.CostEstimate(
            flops=6 * slots * vocab_rows * width,
            bytes_accessed=2 * (vocab_rows + count) * width,
            transcendentals=slots * vocab_rows,
        ),
        name="loss_and_gradient",
    )(kept_count, loss_mask.reshape(1, count), targets.reshape(1, count), hidden, out_weight)
    chosen = lax.broadcasted_iota(jnp.int32, (count, 1), 0) == pos[0, 0]
    hidden_grad = jnp.where(chosen, row_grad, 0.0).astype(jnp.bfloat16)
    return hidden_grad, row_loss.reshape(count)


def shards(hidden, out_weight, loss_mask, targets, kept_count):
    order_pos = jnp.cumsum(loss_mask) - 1
    kept_row = (loss_mask == 1) & (order_pos < kept_count[0])
    slot_ids = jnp.arange(CAP, dtype=jnp.int32)
    slot_hits = kept_row[None, :] & (order_pos[None, :] == slot_ids[:, None])
    packed = jnp.dot(
        slot_hits.astype(jnp.bfloat16), hidden, preferred_element_type=jnp.float32
    ).astype(jnp.bfloat16)
    slot_target = jnp.sum(jnp.where(slot_hits, targets[None, :], 0), axis=1)
    packed_target = jnp.where(jnp.any(slot_hits, axis=1), slot_target, -1)
    gathered, gathered_target = (
        lax.all_gather(packed, ("dp", "tensor"), axis=0, tiled=True),
        lax.all_gather(packed_target, ("dp", "tensor"), axis=0, tiled=True),
    )
    filled = gathered_target >= 0
    vocab_rows = out_weight.shape[0]
    device_pos = lax.axis_index(("dp", "tensor"))
    vocab_ids = device_pos * vocab_rows + jnp.arange(vocab_rows, dtype=jnp.int32)
    logits = jnp.einsum("rd,vd->rv", gathered, out_weight, preferred_element_type=jnp.float32)
    target_hit = vocab_ids[None, :] == gathered_target[:, None]
    local_top = jnp.max(logits, axis=1)
    local_pick = jnp.sum(jnp.where(target_hit, logits, 0.0), axis=1)
    row_top = lax.pmax(local_top, ("dp", "tensor"))
    shifted_total = jnp.sum(jnp.exp(logits - row_top[:, None]), axis=1)
    row_total, picked = lax.psum((shifted_total, local_pick), ("dp", "tensor"))
    log_total = row_top + jnp.log(row_total)
    slot_loss = jnp.where(filled, log_total - picked, 0.0)
    probabilities = jnp.exp(logits - log_total[:, None])
    coefficient = jnp.where(
        filled[:, None], probabilities - target_hit.astype(jnp.float32), 0.0
    ).astype(jnp.bfloat16)
    dp_count = lax.axis_size("dp")
    tensor_count = lax.axis_size("tensor")
    grad_term = jnp.dot(coefficient, out_weight, preferred_element_type=jnp.float32)
    grad_term = grad_term.reshape(dp_count, tensor_count, CAP, grad_term.shape[1])
    partial_sum = lax.psum_scatter(grad_term, "tensor", scatter_dimension=1, tiled=True)
    own_grad = lax.psum_scatter(partial_sum, "dp", scatter_dimension=0, tiled=True)
    own_grad = own_grad.reshape(CAP, own_grad.shape[3])
    own_grad = own_grad * loss_scale
    own_loss = lax.dynamic_slice_in_dim(slot_loss, device_pos * CAP, CAP, 0)
    slot_pos = jnp.clip(order_pos, 0, CAP - 1)
    hidden_grad = jnp.where(kept_row[:, None], own_grad[slot_pos], 0.0).astype(jnp.bfloat16)
    row_loss = jnp.where(kept_row, own_loss[slot_pos], 0.0)
    return (hidden_grad, row_loss)


def fits(mesh, hidden, out_weight):
    devices = mesh.shape["dp"] * mesh.shape["tensor"]
    return (
        mesh.shape["dp"] % CORES == 0
        and mesh.shape["dp"] > CORES
        and mesh.shape["tensor"] > 1
        and devices <= 32
        and hidden.shape[1] <= 8192
        and hidden.shape[1] % (PIECES * 128) == 0
        and out_weight.shape[0] < 2**24
        and out_weight.shape[0] % (devices * 8) == 0
        and out_weight.shape[0] // devices > TILE
    )


def solution(mesh):
    in_specs = (
        P(("dp", "tensor"), None),
        P(("dp", "tensor"), None),
        P(("dp", "tensor")),
        P(("dp", "tensor")),
        P(("dp", "tensor")),
    )
    out_specs = (P(("dp", "tensor"), None), P(("dp", "tensor")))

    def run(hidden, out_weight, loss_mask, targets, kept_count):
        body = fused_shards if fits(mesh, hidden, out_weight) else shards
        mapped = jax.shard_map(
            body, mesh=mesh, in_specs=in_specs, out_specs=out_specs, check_vma=False
        )
        return mapped(hidden, out_weight, loss_mask, targets, kept_count)

    return run
```

```python
import functools

import jax
import jax.numpy as jnp
from jax import lax
from jax.experimental import pallas as pl
from jax.experimental.pallas import tpu as pltpu
from jax.sharding import PartitionSpec as P

CAP = 1


loss_scale = 128.0

CORES = 2
PIECES = 16
TILE = 512
RING = 5
LOW = -1e30


def kernel(
    sizes, kept_ref, mask_ref, target_ref, hidden_ref, weight_ref,
    grad_ref, loss_ref, pos_ref,
    rows, ring, gathered, wide, packed, acc, hit_acc,
    sums, hits, stats,
    core_sums, core_hits, core_stats,
    group_out, group_in, group_stats,
    column_out, column_in, column_stats, column_own,
    rows_sem, ring_sem, send_sem, recv_sem,
):
    chips, depth, vocab_rows, width = sizes
    half = chips * depth
    slots = CORES * half
    piece = width // PIECES
    tiles = -(-vocab_rows // TILE)
    tail = vocab_rows - (tiles - 1) * TILE
    f32, bf16 = jnp.float32, jnp.bfloat16

    dp = lax.axis_index("dp")
    z = lax.axis_index("tensor")
    chip = dp // CORES
    core = dp % CORES
    slot = core * half + chip * depth + z

    def tile_copy(j):
        at = lax.rem(j, RING)
        first = pl.multiple_of((j - 1) * TILE, TILE)
        return pltpu.make_async_copy(
            weight_ref.at[pl.ds(first, TILE)], ring.at[at], ring_sem.at[at]
        )

    tail_copy = pltpu.make_async_copy(
        weight_ref.at[pl.ds((tiles - 1) * TILE, tail)],
        ring.at[0, pl.ds(0, tail)],
        ring_sem.at[0],
    )
    rows_copy = pltpu.make_async_copy(hidden_ref, rows, rows_sem)
    rows_copy.start()
    if tail < TILE:
        zero_from = tail // 16 * 16
        ring[0, zero_from:, :] = jnp.zeros((TILE - zero_from, width), bf16)
    tail_copy.start()
    for j in range(1, min(RING, tiles)):
        tile_copy(j).start()

    chip_peers = [lax.rem(chip + k, chips) for k in range(1, chips)]
    chip_froms = [lax.rem(chip + chips - k, chips) for k in range(1, chips)]
    depth_peers = [lax.rem(z + k, depth) for k in range(1, depth)]
    depth_froms = [lax.rem(z + depth - k, depth) for k in range(1, depth)]
    other = 1 - core

    def to_depth(peer):
        return (dp, peer)

    def to_chip(peer):
        return (peer * CORES + core, z)

    to_core = (chip * CORES + other, z)
    everyone = [to_depth(p) for p in depth_peers] + [to_chip(p) for p in chip_peers] + [to_core]
    barrier = pltpu.get_barrier_semaphore()
    for peer in everyone:
        pl.semaphore_signal(barrier, inc=1, device_id=peer, device_id_type=pl.DeviceIdType.MESH)

    mask = mask_ref[...]
    lanes = lax.broadcasted_iota(jnp.int32, mask.shape, 1)
    count = mask.shape[1]
    kept = kept_ref[0]
    first = jnp.min(jnp.where(mask == 1, lanes, count), axis=1, keepdims=True)
    first = jnp.where(kept > 0, first, count)
    hit = lanes == first
    filled = first < count
    target = jnp.sum(jnp.where(hit, target_ref[...], 0), axis=1, keepdims=True)
    digits = (
        jnp.where(filled, target & 255, -1),
        jnp.where(filled, (target >> 8) & 255, 0),
        jnp.where(filled, target >> 16, 0),
    )
    piece_row = lax.broadcasted_iota(jnp.int32, (PIECES, 128), 0)
    coded = jnp.zeros((PIECES, 128), jnp.int32)
    for k, digit in enumerate(digits):
        coded = jnp.where(piece_row == k, digit, coded)
    own_rows = pl.ds(pl.multiple_of(slot * PIECES, PIECES), PIECES)
    gathered[own_rows, piece:] = coded.astype(f32).astype(bf16)
    select_row = lax.broadcasted_iota(jnp.int32, (PIECES, count), 0)
    hit_rows = jnp.broadcast_to(hit.astype(f32), (PIECES, count))
    rows_copy.wait()
    own = jnp.zeros((PIECES, piece), f32)
    for a in range(PIECES):
        chosen = jnp.where(select_row == a, hit_rows, 0.0).astype(bf16)
        own += jnp.dot(chosen, rows[:, a * piece:(a + 1) * piece], preferred_element_type=f32)
    gathered[own_rows, :piece] = own.astype(bf16)

    started = []
    next_sem = [0]

    def send(src, dst, peer):
        k = next_sem[0]
        next_sem[0] += 1
        copy = pltpu.make_async_remote_copy(
            src_ref=src, dst_ref=dst, send_sem=send_sem.at[k], recv_sem=recv_sem.at[k],
            device_id=peer, device_id_type=pl.DeviceIdType.MESH,
        )
        copy.start()
        started.append(copy)
        return copy

    pl.semaphore_wait(barrier, len(everyone))
    part = gathered.at[own_rows]
    for copy in [send(part, part, to_depth(p)) for p in depth_peers]:
        copy.wait_recv()
    first_row = pl.multiple_of((core * half + chip * depth) * PIECES, PIECES)
    part = gathered.at[pl.ds(first_row, depth * PIECES)]
    for copy in [send(part, part, to_chip(p)) for p in chip_peers]:
        copy.wait_recv()
    first_row = pl.multiple_of(core * (half * PIECES), PIECES)
    part = gathered.at[pl.ds(first_row, half * PIECES)]
    send(part, part, to_core).wait_recv()

    lane_blocks = piece // 128
    for b in range(lane_blocks + 1):
        wide[b] = gathered[:, b * 128:(b + 1) * 128].astype(f32)
    for a in range(PIECES):
        for b in range(lane_blocks):
            low = a * piece + b * 128
            packed[low:low + 128, :] = wide[b, pl.ds(a, slots, stride=PIECES), :].T.astype(bf16)
    code = [wide[lane_blocks, pl.ds(k, slots, stride=PIECES), :] for k in range(3)]
    slot_target = (code[0] + 256.0 * code[1] + 65536.0 * code[2]).astype(jnp.int32)[:, :1]
    acc[...] = jnp.zeros_like(acc)
    hit_acc[...] = jnp.zeros_like(hit_acc)

    vocab_first = (dp * depth + z) * vocab_rows
    columns = lax.broadcasted_iota(jnp.int32, (slots, TILE), 1)

    def logits_of(at):
        return jnp.dot(ring[at], packed[...], preferred_element_type=f32).T

    def absorb(j, logits, top, total, picked):
        at = lax.rem(j, RING)
        begin = jnp.where(j == 0, tiles - 1, j - 1) * TILE
        size = jnp.where(j == 0, tail, TILE)
        valid = columns < size
        logits = jnp.where(valid, logits, LOW)
        here = valid & (columns + (vocab_first + begin) == slot_target)
        later_top = jnp.maximum(top, jnp.max(logits, axis=1, keepdims=True))
        fade = jnp.exp(top - later_top)
        weights = jnp.exp(logits - later_top)
        total = total * fade + jnp.sum(weights, axis=1, keepdims=True)
        picked = picked + jnp.sum(jnp.where(here, logits, 0.0), axis=1, keepdims=True)
        both = jnp.concatenate(
            [jnp.where(here, 0.0, weights), here.astype(f32)], axis=0
        ).astype(bf16)
        for a in range(PIECES):
            cut = slice(a * piece, (a + 1) * piece)
            term = jnp.dot(both, ring[at, :, cut], preferred_element_type=f32)
            acc[:, cut] = acc[:, cut] * fade + term[:slots]
            hit_acc[:, cut] += term[slots:]
        return later_top, total, picked

    def step(j, carry):
        logits, top, total, picked = carry
        tile_copy(j + 1).wait()
        later = logits_of(lax.rem(j + 1, RING))
        top, total, picked = absorb(j, logits, top, total, picked)

        @pl.when(j + RING < tiles)
        def _():
            tile_copy(j + RING).start()

        return later, top, total, picked

    tail_copy.wait()
    start = jnp.zeros((slots, 1), f32)
    carry = (logits_of(0), start + LOW, start, start)
    carry = lax.fori_loop(0, tiles - 1, step, carry)
    top, total, picked = absorb(jnp.int32(tiles - 1), *carry)

    def by_slot(source):
        for a in range(PIECES):
            for b in range(lane_blocks):
                low = a * piece + b * 128
                wide[b, pl.ds(a, slots, stride=PIECES), :] = source[:, low:low + 128]

    by_slot(acc)
    for b in range(lane_blocks):
        sums[:, b * 128:(b + 1) * 128] = wide[b]
    by_slot(hit_acc)
    for b in range(lane_blocks):
        hits[:, b * 128:(b + 1) * 128] = wide[b].astype(bf16)
    stats[...] = jnp.zeros_like(stats)
    for k, value in enumerate((top, total, picked)):
        stats[pl.ds(k, slots, stride=8), :] = jnp.broadcast_to(value, (slots, 128))

    def merge(parts):
        tops = [s[0:1] for _, _, s in parts]
        top = functools.reduce(jnp.maximum, tops)
        fades = [jnp.exp(t - top) for t in tops]
        total = sum(f * s[1:2] for f, (_, _, s) in zip(fades, parts))
        picked = sum(s[2:3] for _, _, s in parts)
        grad = sum(
            jnp.concatenate([f] * lane_blocks, axis=1) * g for f, (g, _, _) in zip(fades, parts)
        )
        target_row = sum(h for _, h, _ in parts)
        return grad, target_row, top, total, picked

    def block_of(top, total, picked):
        row = lax.broadcasted_iota(jnp.int32, (8, 128), 0)
        zero = jnp.zeros((8, 128), f32)
        return jnp.where(row == 0, top, jnp.where(row == 1, total, jnp.where(row == 2, picked, zero)))

    theirs = pl.multiple_of(other * (half * PIECES), PIECES)
    their_stats = pl.multiple_of(other * (half * 8), 8)
    copies = [
        send(stats.at[pl.ds(their_stats, half * 8)], core_stats, to_core),
        send(sums.at[pl.ds(theirs, half * PIECES)], core_sums, to_core),
        send(hits.at[pl.ds(theirs, half * PIECES)], core_hits, to_core),
    ]
    for copy in copies:
        copy.wait_recv()
    mine = pl.multiple_of(core * (half * PIECES), PIECES)
    mine_stats = pl.multiple_of(core * (half * 8), 8)

    def core_merge(s, _):
        at = pl.ds(pl.multiple_of(mine + s * PIECES, PIECES), PIECES)
        at_stats = pl.ds(pl.multiple_of(mine_stats + s * 8, 8), 8)
        there = pl.ds(pl.multiple_of(s * PIECES, PIECES), PIECES)
        there_stats = pl.ds(pl.multiple_of(s * 8, 8), 8)
        grad, target_row, *rest = merge([
            (sums[at], hits[at].astype(f32), stats[at_stats]),
            (core_sums[there], core_hits[there].astype(f32), core_stats[there_stats]),
        ])
        core_sums[there] = grad
        core_stats[there_stats] = block_of(*rest)
        lower = pl.multiple_of(s * (2 * PIECES), PIECES)
        group_out[pl.ds(lower, PIECES)] = grad.astype(bf16)
        group_out[pl.ds(lower + PIECES, PIECES)] = target_row.astype(bf16)
        return 0

    lax.fori_loop(0, half, core_merge, 0, unroll=4)

    span = depth * 2 * PIECES
    copies = []
    for k, peer in enumerate(chip_peers):
        copies.append(send(
            core_stats.at[pl.ds(pl.multiple_of(peer * (depth * 8), 8), depth * 8)],
            group_stats.at[k], to_chip(peer),
        ))
        copies.append(send(
            group_out.at[pl.ds(pl.multiple_of(peer * span, PIECES), span)],
            group_in.at[k], to_chip(peer),
        ))
    for copy in copies:
        copy.wait_recv()
    for s in range(depth):
        at = pl.ds(pl.multiple_of((chip * depth + s) * PIECES, PIECES), PIECES)
        at_stats = pl.ds(pl.multiple_of((chip * depth + s) * 8, 8), 8)
        own_hit = pl.ds(pl.multiple_of((chip * depth + s) * (2 * PIECES) + PIECES, PIECES), PIECES)
        low = s * 2 * PIECES
        parts = [(core_sums[at], group_out[own_hit].astype(f32), core_stats[at_stats])]
        for k in range(chips - 1):
            parts.append((
                group_in[k, low:low + PIECES].astype(f32),
                group_in[k, low + PIECES:low + 2 * PIECES].astype(f32),
                group_stats[k, s * 8:s * 8 + 8],
            ))
        grad, target_row, *rest = merge(parts)
        core_sums[at] = grad
        column_own[s * 8:s * 8 + 8] = block_of(*rest)
        column_out[low:low + PIECES] = grad.astype(bf16)
        column_out[low + PIECES:low + 2 * PIECES] = target_row.astype(bf16)

    copies = []
    for k, peer in enumerate(depth_peers):
        copies.append(send(
            column_own.at[pl.ds(pl.multiple_of(peer * 8, 8), 8)], column_stats.at[k], to_depth(peer)
        ))
        copies.append(send(
            column_out.at[pl.ds(pl.multiple_of(peer * (2 * PIECES), PIECES), 2 * PIECES)],
            column_in.at[k], to_depth(peer),
        ))
    for copy in copies:
        copy.wait_recv()
    parts = [(
        core_sums[pl.ds(pl.multiple_of((chip * depth + z) * PIECES, PIECES), PIECES)],
        column_out[pl.ds(pl.multiple_of(z * (2 * PIECES) + PIECES, PIECES), PIECES)].astype(f32),
        column_own[pl.ds(pl.multiple_of(z * 8, 8), 8)],
    )]
    for k in range(depth - 1):
        parts.append((
            column_in[k, :PIECES].astype(f32), column_in[k, PIECES:].astype(f32), column_stats[k]
        ))
    grad, target_row, top, total, picked = merge(parts)
    log_total = top + jnp.log(total)
    share = jnp.concatenate([1.0 / total] * lane_blocks, axis=1)
    at_target = (jnp.exp(picked - log_total) - 1.0).astype(bf16).astype(f32)
    at_target = jnp.concatenate([at_target] * lane_blocks, axis=1)
    grad = (grad * share + target_row * at_target) * loss_scale
    for a in range(PIECES):
        grad_ref[:, a * piece:(a + 1) * piece] = grad[a:a + 1]
    loss_ref[...] = jnp.where(hit, (log_total - picked)[:, :1], 0.0)
    pos_ref[...] = jnp.broadcast_to(first, pos_ref.shape)
    for copy in started:
        copy.wait_send()


def spread(grad_ref, loss_ref, pos_ref, hidden_grad_ref, row_loss_ref):
    rows, lanes = hidden_grad_ref.shape
    chosen = lax.broadcasted_iota(jnp.int32, (rows, lanes), 0) == pos_ref[:, :1]
    hidden_grad_ref[...] = jnp.where(chosen, grad_ref[...], 0.0).astype(hidden_grad_ref.dtype)
    row_loss_ref[...] = loss_ref[0, :]


def fused_shards(hidden, out_weight, loss_mask, targets, kept_count):
    count, width = hidden.shape
    vocab_rows = out_weight.shape[0]
    chips = lax.axis_size("dp") // CORES
    depth = lax.axis_size("tensor")
    half = chips * depth
    slots = CORES * half
    piece = width // PIECES
    f32, bf16 = jnp.float32, jnp.bfloat16
    copies = 2 * (depth - 1) + 2 * (chips - 1) + (chips - 1) + (depth - 1) + 4
    vmem, any_space = pl.BlockSpec(memory_space=pltpu.VMEM), pl.BlockSpec(memory_space=pl.ANY)
    row_grad, row_loss, pos = pl.pallas_call(
        functools.partial(kernel, (chips, depth, vocab_rows, width)),
        out_shape=(
            jax.ShapeDtypeStruct((1, width), f32),
            jax.ShapeDtypeStruct((1, count), f32),
            jax.ShapeDtypeStruct((1, count), jnp.int32),
        ),
        in_specs=[pl.BlockSpec(memory_space=pltpu.SMEM), vmem, vmem, any_space, any_space],
        out_specs=(vmem, vmem, vmem),
        scratch_shapes=[
            pltpu.VMEM((count, width), bf16),
            pltpu.VMEM((RING, TILE, width), bf16),
            pltpu.VMEM((slots * PIECES, piece + 128), bf16),
            pltpu.VMEM((piece // 128 + 1, slots * PIECES, 128), f32),
            pltpu.VMEM((width, slots), bf16),
            pltpu.VMEM((slots, width), f32),
            pltpu.VMEM((slots, width), f32),
            pltpu.VMEM((slots * PIECES, piece), f32),
            pltpu.VMEM((slots * PIECES, piece), bf16),
            pltpu.VMEM((slots * 8, 128), f32),
            pltpu.VMEM((half * PIECES, piece), f32),
            pltpu.VMEM((half * PIECES, piece), bf16),
            pltpu.VMEM((half * 8, 128), f32),
            pltpu.VMEM((half * 2 * PIECES, piece), bf16),
            pltpu.VMEM((chips - 1, depth * 2 * PIECES, piece), bf16),
            pltpu.VMEM((chips - 1, depth * 8, 128), f32),
            pltpu.VMEM((depth * 2 * PIECES, piece), bf16),
            pltpu.VMEM((depth - 1, 2 * PIECES, piece), bf16),
            pltpu.VMEM((depth - 1, 8, 128), f32),
            pltpu.VMEM((depth * 8, 128), f32),
            pltpu.SemaphoreType.DMA,
            pltpu.SemaphoreType.DMA((RING,)),
            pltpu.SemaphoreType.DMA((copies,)),
            pltpu.SemaphoreType.DMA((copies,)),
        ],
        compiler_params=pltpu.CompilerParams(
            collective_id=0, has_side_effects=True, vmem_limit_bytes=60 * 2**20
        ),
        cost_estimate=pl.CostEstimate(
            flops=6 * slots * vocab_rows * width,
            bytes_accessed=2 * (vocab_rows + count) * width,
            transcendentals=slots * vocab_rows,
        ),
        name="loss_and_gradient",
    )(kept_count, loss_mask.reshape(1, count), targets.reshape(1, count), hidden, out_weight)
    return pl.pallas_call(
        spread,
        out_shape=(
            jax.ShapeDtypeStruct((count, width), bf16),
            jax.ShapeDtypeStruct((count,), f32),
        ),
        grid=(8,),
        in_specs=[
            pl.BlockSpec((1, width // 8), lambda i: (0, i)),
            pl.BlockSpec((1, count), lambda i: (0, 0)),
            pl.BlockSpec((1, count), lambda i: (0, 0)),
        ],
        out_specs=(
            pl.BlockSpec((count, width // 8), lambda i: (0, i)),
            pl.BlockSpec((count,), lambda i: (0,)),
        ),
        name="spread",
    )(row_grad, row_loss, pos)


def shards(hidden, out_weight, loss_mask, targets, kept_count):
    order_pos = jnp.cumsum(loss_mask) - 1
    kept_row = (loss_mask == 1) & (order_pos < kept_count[0])
    slot_ids = jnp.arange(CAP, dtype=jnp.int32)
    slot_hits = kept_row[None, :] & (order_pos[None, :] == slot_ids[:, None])
    packed = jnp.dot(
        slot_hits.astype(jnp.bfloat16), hidden, preferred_element_type=jnp.float32
    ).astype(jnp.bfloat16)
    slot_target = jnp.sum(jnp.where(slot_hits, targets[None, :], 0), axis=1)
    packed_target = jnp.where(jnp.any(slot_hits, axis=1), slot_target, -1)
    gathered, gathered_target = (
        lax.all_gather(packed, ("dp", "tensor"), axis=0, tiled=True),
        lax.all_gather(packed_target, ("dp", "tensor"), axis=0, tiled=True),
    )
    filled = gathered_target >= 0
    vocab_rows = out_weight.shape[0]
    device_pos = lax.axis_index(("dp", "tensor"))
    vocab_ids = device_pos * vocab_rows + jnp.arange(vocab_rows, dtype=jnp.int32)
    logits = jnp.einsum("rd,vd->rv", gathered, out_weight, preferred_element_type=jnp.float32)
    target_hit = vocab_ids[None, :] == gathered_target[:, None]
    local_top = jnp.max(logits, axis=1)
    local_pick = jnp.sum(jnp.where(target_hit, logits, 0.0), axis=1)
    row_top = lax.pmax(local_top, ("dp", "tensor"))
    shifted_total = jnp.sum(jnp.exp(logits - row_top[:, None]), axis=1)
    row_total, picked = lax.psum((shifted_total, local_pick), ("dp", "tensor"))
    log_total = row_top + jnp.log(row_total)
    slot_loss = jnp.where(filled, log_total - picked, 0.0)
    probabilities = jnp.exp(logits - log_total[:, None])
    coefficient = jnp.where(
        filled[:, None], probabilities - target_hit.astype(jnp.float32), 0.0
    ).astype(jnp.bfloat16)
    dp_count = lax.axis_size("dp")
    tensor_count = lax.axis_size("tensor")
    grad_term = jnp.dot(coefficient, out_weight, preferred_element_type=jnp.float32)
    grad_term = grad_term.reshape(dp_count, tensor_count, CAP, grad_term.shape[1])
    partial_sum = lax.psum_scatter(grad_term, "tensor", scatter_dimension=1, tiled=True)
    own_grad = lax.psum_scatter(partial_sum, "dp", scatter_dimension=0, tiled=True)
    own_grad = own_grad.reshape(CAP, own_grad.shape[3])
    own_grad = own_grad * loss_scale
    own_loss = lax.dynamic_slice_in_dim(slot_loss, device_pos * CAP, CAP, 0)
    slot_pos = jnp.clip(order_pos, 0, CAP - 1)
    hidden_grad = jnp.where(kept_row[:, None], own_grad[slot_pos], 0.0).astype(jnp.bfloat16)
    row_loss = jnp.where(kept_row, own_loss[slot_pos], 0.0)
    return (hidden_grad, row_loss)


def fits(mesh, hidden, out_weight):
    devices = mesh.shape["dp"] * mesh.shape["tensor"]
    return (
        mesh.shape["dp"] % CORES == 0
        and mesh.shape["dp"] > CORES
        and mesh.shape["tensor"] > 1
        and devices <= 32
        and hidden.shape[1] <= 8192
        and hidden.shape[1] % (PIECES * 128) == 0
        and out_weight.shape[0] < 2**24
        and out_weight.shape[0] % (devices * 8) == 0
        and out_weight.shape[0] // devices > TILE
    )


def solution(mesh):
    in_specs = (
        P(("dp", "tensor"), None),
        P(("dp", "tensor"), None),
        P(("dp", "tensor")),
        P(("dp", "tensor")),
        P(("dp", "tensor")),
    )
    out_specs = (P(("dp", "tensor"), None), P(("dp", "tensor")))

    def run(hidden, out_weight, loss_mask, targets, kept_count):
        body = fused_shards if fits(mesh, hidden, out_weight) else shards
        mapped = jax.shard_map(
            body, mesh=mesh, in_specs=in_specs, out_specs=out_specs, check_vma=False
        )
        return mapped(hidden, out_weight, loss_mask, targets, kept_count)

    return run
```

```python
import functools

import jax
import jax.numpy as jnp
from jax import lax
from jax.experimental import pallas as pl
from jax.experimental.pallas import tpu as pltpu
from jax.sharding import PartitionSpec as P

CAP = 1


loss_scale = 128.0

CORES = 2
PIECES = 16
TILE = 512
RING = 5
LOW = -1e30


def kernel(
    sizes, kept_ref, mask_ref, target_ref, hidden_ref, weight_ref,
    grad_ref, loss_ref, pos_ref,
    rows, ring, gathered, wide, packed, acc, hit_acc,
    sums, hits, stats,
    core_sums, core_hits, core_stats,
    group_out, group_in, group_stats,
    column_out, column_in, column_stats, column_own,
    rows_sem, ring_sem, send_sem, recv_sem,
):
    chips, depth, vocab_rows, width = sizes
    half = chips * depth
    slots = CORES * half
    piece = width // PIECES
    tiles = -(-vocab_rows // TILE)
    tail = vocab_rows - (tiles - 1) * TILE
    f32, bf16 = jnp.float32, jnp.bfloat16

    dp = lax.axis_index("dp")
    z = lax.axis_index("tensor")
    chip = dp // CORES
    core = dp % CORES
    slot = core * half + chip * depth + z

    def tile_copy(j):
        at = lax.rem(j, RING)
        first = pl.multiple_of((j - 1) * TILE, TILE)
        return pltpu.make_async_copy(
            weight_ref.at[pl.ds(first, TILE)], ring.at[at], ring_sem.at[at]
        )

    tail_copy = pltpu.make_async_copy(
        weight_ref.at[pl.ds((tiles - 1) * TILE, tail)],
        ring.at[0, pl.ds(0, tail)],
        ring_sem.at[0],
    )
    rows_copy = pltpu.make_async_copy(hidden_ref, rows, rows_sem)
    rows_copy.start()
    if tail < TILE:
        zero_from = tail // 16 * 16
        ring[0, zero_from:, :] = jnp.zeros((TILE - zero_from, width), bf16)
    tail_copy.start()
    for j in range(1, min(RING, tiles)):
        tile_copy(j).start()

    chip_peers = [lax.rem(chip + k, chips) for k in range(1, chips)]
    chip_froms = [lax.rem(chip + chips - k, chips) for k in range(1, chips)]
    depth_peers = [lax.rem(z + k, depth) for k in range(1, depth)]
    depth_froms = [lax.rem(z + depth - k, depth) for k in range(1, depth)]
    other = 1 - core

    def to_depth(peer):
        return (dp, peer)

    def to_chip(peer):
        return (peer * CORES + core, z)

    to_core = (chip * CORES + other, z)
    everyone = [to_depth(p) for p in depth_peers] + [to_chip(p) for p in chip_peers] + [to_core]
    barrier = pltpu.get_barrier_semaphore()
    for peer in everyone:
        pl.semaphore_signal(barrier, inc=1, device_id=peer, device_id_type=pl.DeviceIdType.MESH)

    mask = mask_ref[...]
    lanes = lax.broadcasted_iota(jnp.int32, mask.shape, 1)
    count = mask.shape[1]
    kept = kept_ref[0]
    first = jnp.min(jnp.where(mask == 1, lanes, count), axis=1, keepdims=True)
    first = jnp.where(kept > 0, first, count)
    hit = lanes == first
    filled = first < count
    target = jnp.sum(jnp.where(hit, target_ref[...], 0), axis=1, keepdims=True)
    digits = (
        jnp.where(filled, target & 255, -1),
        jnp.where(filled, (target >> 8) & 255, 0),
        jnp.where(filled, target >> 16, 0),
    )
    piece_row = lax.broadcasted_iota(jnp.int32, (PIECES, 128), 0)
    coded = jnp.zeros((PIECES, 128), jnp.int32)
    for k, digit in enumerate(digits):
        coded = jnp.where(piece_row == k, digit, coded)
    own_rows = pl.ds(pl.multiple_of(slot * PIECES, PIECES), PIECES)
    gathered[own_rows, piece:] = coded.astype(f32).astype(bf16)
    select_row = lax.broadcasted_iota(jnp.int32, (PIECES, count), 0)
    hit_rows = jnp.broadcast_to(hit.astype(f32), (PIECES, count))
    rows_copy.wait()
    own = jnp.zeros((PIECES, piece), f32)
    for a in range(PIECES):
        chosen = jnp.where(select_row == a, hit_rows, 0.0).astype(bf16)
        own += jnp.dot(chosen, rows[:, a * piece:(a + 1) * piece], preferred_element_type=f32)
    gathered[own_rows, :piece] = own.astype(bf16)

    started = []
    next_sem = [0]

    def send(src, dst, peer):
        k = next_sem[0]
        next_sem[0] += 1
        copy = pltpu.make_async_remote_copy(
            src_ref=src, dst_ref=dst, send_sem=send_sem.at[k], recv_sem=recv_sem.at[k],
            device_id=peer, device_id_type=pl.DeviceIdType.MESH,
        )
        copy.start()
        started.append(copy)
        return copy

    pl.semaphore_wait(barrier, len(everyone))
    part = gathered.at[own_rows]
    from_column = [send(part, part, to_depth(p)) for p in depth_peers]
    from_chips = [[send(part, part, to_chip(p))] for p in chip_peers]
    for copy, source in zip(from_column, depth_froms):
        copy.wait_recv()
        first_row = pl.multiple_of((core * half + chip * depth + source) * PIECES, PIECES)
        part = gathered.at[pl.ds(first_row, PIECES)]
        for copies, peer in zip(from_chips, chip_peers):
            copies.append(send(part, part, to_chip(peer)))
    from_core = []
    for copies, source in zip([[]] + from_chips, [chip] + chip_froms):
        for copy in copies:
            copy.wait_recv()
        first_row = pl.multiple_of((core * half + source * depth) * PIECES, PIECES)
        part = gathered.at[pl.ds(first_row, depth * PIECES)]
        from_core.append(send(part, part, to_core))
    for copy in from_core:
        copy.wait_recv()

    lane_blocks = piece // 128
    for b in range(lane_blocks + 1):
        wide[b] = gathered[:, b * 128:(b + 1) * 128].astype(f32)
    for a in range(PIECES):
        for b in range(lane_blocks):
            low = a * piece + b * 128
            packed[low:low + 128, :] = wide[b, pl.ds(a, slots, stride=PIECES), :].T.astype(bf16)
    code = [wide[lane_blocks, pl.ds(k, slots, stride=PIECES), :] for k in range(3)]
    slot_target = (code[0] + 256.0 * code[1] + 65536.0 * code[2]).astype(jnp.int32)[:, :1]
    acc[...] = jnp.zeros_like(acc)
    hit_acc[...] = jnp.zeros_like(hit_acc)

    vocab_first = (dp * depth + z) * vocab_rows
    columns = lax.broadcasted_iota(jnp.int32, (slots, TILE), 1)

    def logits_of(at):
        return jnp.dot(ring[at], packed[...], preferred_element_type=f32).T

    def absorb(j, logits, top, total, picked):
        at = lax.rem(j, RING)
        begin = jnp.where(j == 0, tiles - 1, j - 1) * TILE
        size = jnp.where(j == 0, tail, TILE)
        valid = columns < size
        logits = jnp.where(valid, logits, LOW)
        here = valid & (columns + (vocab_first + begin) == slot_target)
        later_top = jnp.maximum(top, jnp.max(logits, axis=1, keepdims=True))
        fade = jnp.exp(top - later_top)
        weights = jnp.exp(logits - later_top)
        total = total * fade + jnp.sum(weights, axis=1, keepdims=True)
        picked = picked + jnp.sum(jnp.where(here, logits, 0.0), axis=1, keepdims=True)
        both = jnp.concatenate(
            [jnp.where(here, 0.0, weights), here.astype(f32)], axis=0
        ).astype(bf16)
        for a in range(PIECES):
            cut = slice(a * piece, (a + 1) * piece)
            term = jnp.dot(both, ring[at, :, cut], preferred_element_type=f32)
            acc[:, cut] = acc[:, cut] * fade + term[:slots]
            hit_acc[:, cut] += term[slots:]
        return later_top, total, picked

    def step(j, carry):
        logits, top, total, picked = carry
        tile_copy(j + 1).wait()
        later = logits_of(lax.rem(j + 1, RING))
        top, total, picked = absorb(j, logits, top, total, picked)

        @pl.when(j + RING < tiles)
        def _():
            tile_copy(j + RING).start()

        return later, top, total, picked

    tail_copy.wait()
    start = jnp.zeros((slots, 1), f32)
    carry = (logits_of(0), start + LOW, start, start)
    carry = lax.fori_loop(0, tiles - 1, step, carry)
    top, total, picked = absorb(jnp.int32(tiles - 1), *carry)

    def by_slot(source):
        for a in range(PIECES):
            for b in range(lane_blocks):
                low = a * piece + b * 128
                wide[b, pl.ds(a, slots, stride=PIECES), :] = source[:, low:low + 128]

    by_slot(acc)
    for b in range(lane_blocks):
        sums[:, b * 128:(b + 1) * 128] = wide[b]
    by_slot(hit_acc)
    for b in range(lane_blocks):
        hits[:, b * 128:(b + 1) * 128] = wide[b].astype(bf16)
    stats[...] = jnp.zeros_like(stats)
    for k, value in enumerate((top, total, picked)):
        stats[pl.ds(k, slots, stride=8), :] = jnp.broadcast_to(value, (slots, 128))

    def merge(parts):
        tops = [s[0:1] for _, _, s in parts]
        top = functools.reduce(jnp.maximum, tops)
        fades = [jnp.exp(t - top) for t in tops]
        total = sum(f * s[1:2] for f, (_, _, s) in zip(fades, parts))
        picked = sum(s[2:3] for _, _, s in parts)
        grad = sum(
            jnp.concatenate([f] * lane_blocks, axis=1) * g for f, (g, _, _) in zip(fades, parts)
        )
        target_row = sum(h for _, h, _ in parts)
        return grad, target_row, top, total, picked

    def block_of(top, total, picked):
        row = lax.broadcasted_iota(jnp.int32, (8, 128), 0)
        zero = jnp.zeros((8, 128), f32)
        return jnp.where(row == 0, top, jnp.where(row == 1, total, jnp.where(row == 2, picked, zero)))

    group_order = chip_peers + [chip]
    slot_order = depth_peers + [z]
    their_stats = pl.multiple_of(other * (half * 8), 8)
    stats_copy = send(stats.at[pl.ds(their_stats, half * 8)], core_stats, to_core)
    core_copies = []
    for group in group_order:
        theirs = pl.multiple_of((other * half + group * depth) * PIECES, PIECES)
        there = pl.ds(pl.multiple_of(group * (depth * PIECES), PIECES), depth * PIECES)
        core_copies.append([
            send(sums.at[pl.ds(theirs, depth * PIECES)], core_sums.at[there], to_core),
            send(hits.at[pl.ds(theirs, depth * PIECES)], core_hits.at[there], to_core),
        ])
    mine = pl.multiple_of(core * (half * PIECES), PIECES)
    mine_stats = pl.multiple_of(core * (half * 8), 8)

    def core_merge(s, _):
        at = pl.ds(pl.multiple_of(mine + s * PIECES, PIECES), PIECES)
        at_stats = pl.ds(pl.multiple_of(mine_stats + s * 8, 8), 8)
        there = pl.ds(pl.multiple_of(s * PIECES, PIECES), PIECES)
        there_stats = pl.ds(pl.multiple_of(s * 8, 8), 8)
        grad, target_row, *rest = merge([
            (sums[at], hits[at].astype(f32), stats[at_stats]),
            (core_sums[there], core_hits[there].astype(f32), core_stats[there_stats]),
        ])
        core_sums[there] = grad
        core_stats[there_stats] = block_of(*rest)
        lower = pl.multiple_of(s * (2 * PIECES), PIECES)
        group_out[pl.ds(lower, PIECES)] = grad.astype(bf16)
        group_out[pl.ds(lower + PIECES, PIECES)] = target_row.astype(bf16)
        return 0

    def group_merge(copies, group):
        for copy in copies:
            copy.wait_recv()
        lax.fori_loop(0, depth, lambda s, c: core_merge(group * depth + s, c), 0, unroll=True)

    stats_copy.wait_recv()
    chip_stats = []
    for k, peer in enumerate(chip_peers):
        group_merge(core_copies[k], peer)
        chip_stats.append(send(
            core_stats.at[pl.ds(pl.multiple_of(peer * (depth * 8), 8), depth * 8)],
            group_stats.at[k], to_chip(peer),
        ))
    from_chips = []
    for s in slot_order:
        low = pl.multiple_of(s * (2 * PIECES), PIECES)
        from_chips.append([
            send(
                group_out.at[pl.ds(
                    pl.multiple_of((peer * depth + s) * (2 * PIECES), PIECES), 2 * PIECES
                )],
                group_in.at[k, pl.ds(low, 2 * PIECES)], to_chip(peer),
            )
            for k, peer in enumerate(chip_peers)
        ])
    group_merge(core_copies[-1], chip)
    for copy in chip_stats:
        copy.wait_recv()

    column_copies = []
    for n, s in enumerate(slot_order):
        for copy in from_chips[n]:
            copy.wait_recv()
        at = pl.ds(pl.multiple_of((chip * depth + s) * PIECES, PIECES), PIECES)
        at_stats = pl.ds(pl.multiple_of((chip * depth + s) * 8, 8), 8)
        own_hit = pl.ds(pl.multiple_of((chip * depth + s) * (2 * PIECES) + PIECES, PIECES), PIECES)
        low = pl.multiple_of(s * (2 * PIECES), PIECES)
        at_own = pl.ds(pl.multiple_of(s * 8, 8), 8)
        parts = [(core_sums[at], group_out[own_hit].astype(f32), core_stats[at_stats])]
        for k in range(chips - 1):
            parts.append((
                group_in[k, pl.ds(low, PIECES)].astype(f32),
                group_in[k, pl.ds(low + PIECES, PIECES)].astype(f32),
                group_stats[k, at_own],
            ))
        grad, target_row, *rest = merge(parts)
        core_sums[at] = grad
        column_own[at_own] = block_of(*rest)
        column_out[pl.ds(low, PIECES)] = grad.astype(bf16)
        column_out[pl.ds(low + PIECES, PIECES)] = target_row.astype(bf16)
        if n < depth - 1:
            column_copies.append(send(column_own.at[at_own], column_stats.at[n], to_depth(s)))
            column_copies.append(send(
                column_out.at[pl.ds(low, 2 * PIECES)], column_in.at[n], to_depth(s)
            ))
    for copy in column_copies:
        copy.wait_recv()
    parts = [(
        core_sums[pl.ds(pl.multiple_of((chip * depth + z) * PIECES, PIECES), PIECES)],
        column_out[pl.ds(pl.multiple_of(z * (2 * PIECES) + PIECES, PIECES), PIECES)].astype(f32),
        column_own[pl.ds(pl.multiple_of(z * 8, 8), 8)],
    )]
    for k in range(depth - 1):
        parts.append((
            column_in[k, :PIECES].astype(f32), column_in[k, PIECES:].astype(f32), column_stats[k]
        ))
    grad, target_row, top, total, picked = merge(parts)
    log_total = top + jnp.log(total)
    share = jnp.concatenate([1.0 / total] * lane_blocks, axis=1)
    at_target = (jnp.exp(picked - log_total) - 1.0).astype(bf16).astype(f32)
    at_target = jnp.concatenate([at_target] * lane_blocks, axis=1)
    grad = (grad * share + target_row * at_target) * loss_scale
    for a in range(PIECES):
        grad_ref[:, a * piece:(a + 1) * piece] = grad[a:a + 1]
    loss_ref[...] = jnp.where(hit, (log_total - picked)[:, :1], 0.0)
    pos_ref[...] = jnp.broadcast_to(first, pos_ref.shape)
    for copy in started:
        copy.wait_send()


def fused_shards(hidden, out_weight, loss_mask, targets, kept_count):
    count, width = hidden.shape
    vocab_rows = out_weight.shape[0]
    chips = lax.axis_size("dp") // CORES
    depth = lax.axis_size("tensor")
    half = chips * depth
    slots = CORES * half
    piece = width // PIECES
    f32, bf16 = jnp.float32, jnp.bfloat16
    copies = 3 * (depth - 1) + (chips - 1) * (2 * depth + 1) + 3 * chips + 1
    vmem, any_space = pl.BlockSpec(memory_space=pltpu.VMEM), pl.BlockSpec(memory_space=pl.ANY)
    row_grad, row_loss, pos = pl.pallas_call(
        functools.partial(kernel, (chips, depth, vocab_rows, width)),
        out_shape=(
            jax.ShapeDtypeStruct((1, width), f32),
            jax.ShapeDtypeStruct((1, count), f32),
            jax.ShapeDtypeStruct((1, count), jnp.int32),
        ),
        in_specs=[pl.BlockSpec(memory_space=pltpu.SMEM), vmem, vmem, any_space, any_space],
        out_specs=(vmem, vmem, vmem),
        scratch_shapes=[
            pltpu.VMEM((count, width), bf16),
            pltpu.VMEM((RING, TILE, width), bf16),
            pltpu.VMEM((slots * PIECES, piece + 128), bf16),
            pltpu.VMEM((piece // 128 + 1, slots * PIECES, 128), f32),
            pltpu.VMEM((width, slots), bf16),
            pltpu.VMEM((slots, width), f32),
            pltpu.VMEM((slots, width), f32),
            pltpu.VMEM((slots * PIECES, piece), f32),
            pltpu.VMEM((slots * PIECES, piece), bf16),
            pltpu.VMEM((slots * 8, 128), f32),
            pltpu.VMEM((half * PIECES, piece), f32),
            pltpu.VMEM((half * PIECES, piece), bf16),
            pltpu.VMEM((half * 8, 128), f32),
            pltpu.VMEM((half * 2 * PIECES, piece), bf16),
            pltpu.VMEM((chips - 1, depth * 2 * PIECES, piece), bf16),
            pltpu.VMEM((chips - 1, depth * 8, 128), f32),
            pltpu.VMEM((depth * 2 * PIECES, piece), bf16),
            pltpu.VMEM((depth - 1, 2 * PIECES, piece), bf16),
            pltpu.VMEM((depth - 1, 8, 128), f32),
            pltpu.VMEM((depth * 8, 128), f32),
            pltpu.SemaphoreType.DMA,
            pltpu.SemaphoreType.DMA((RING,)),
            pltpu.SemaphoreType.DMA((copies,)),
            pltpu.SemaphoreType.DMA((copies,)),
        ],
        compiler_params=pltpu.CompilerParams(
            collective_id=0, has_side_effects=True, vmem_limit_bytes=60 * 2**20
        ),
        cost_estimate=pl.CostEstimate(
            flops=6 * slots * vocab_rows * width,
            bytes_accessed=2 * (vocab_rows + count) * width,
            transcendentals=slots * vocab_rows,
        ),
        name="loss_and_gradient",
    )(kept_count, loss_mask.reshape(1, count), targets.reshape(1, count), hidden, out_weight)
    chosen = lax.broadcasted_iota(jnp.int32, (count, 1), 0) == pos[0, 0]
    hidden_grad = jnp.where(chosen, row_grad, 0.0).astype(bf16)
    return hidden_grad, row_loss.reshape(count)


def shards(hidden, out_weight, loss_mask, targets, kept_count):
    order_pos = jnp.cumsum(loss_mask) - 1
    kept_row = (loss_mask == 1) & (order_pos < kept_count[0])
    slot_ids = jnp.arange(CAP, dtype=jnp.int32)
    slot_hits = kept_row[None, :] & (order_pos[None, :] == slot_ids[:, None])
    packed = jnp.dot(
        slot_hits.astype(jnp.bfloat16), hidden, preferred_element_type=jnp.float32
    ).astype(jnp.bfloat16)
    slot_target = jnp.sum(jnp.where(slot_hits, targets[None, :], 0), axis=1)
    packed_target = jnp.where(jnp.any(slot_hits, axis=1), slot_target, -1)
    gathered, gathered_target = (
        lax.all_gather(packed, ("dp", "tensor"), axis=0, tiled=True),
        lax.all_gather(packed_target, ("dp", "tensor"), axis=0, tiled=True),
    )
    filled = gathered_target >= 0
    vocab_rows = out_weight.shape[0]
    device_pos = lax.axis_index(("dp", "tensor"))
    vocab_ids = device_pos * vocab_rows + jnp.arange(vocab_rows, dtype=jnp.int32)
    logits = jnp.einsum("rd,vd->rv", gathered, out_weight, preferred_element_type=jnp.float32)
    target_hit = vocab_ids[None, :] == gathered_target[:, None]
    local_top = jnp.max(logits, axis=1)
    local_pick = jnp.sum(jnp.where(target_hit, logits, 0.0), axis=1)
    row_top = lax.pmax(local_top, ("dp", "tensor"))
    shifted_total = jnp.sum(jnp.exp(logits - row_top[:, None]), axis=1)
    row_total, picked = lax.psum((shifted_total, local_pick), ("dp", "tensor"))
    log_total = row_top + jnp.log(row_total)
    slot_loss = jnp.where(filled, log_total - picked, 0.0)
    probabilities = jnp.exp(logits - log_total[:, None])
    coefficient = jnp.where(
        filled[:, None], probabilities - target_hit.astype(jnp.float32), 0.0
    ).astype(jnp.bfloat16)
    dp_count = lax.axis_size("dp")
    tensor_count = lax.axis_size("tensor")
    grad_term = jnp.dot(coefficient, out_weight, preferred_element_type=jnp.float32)
    grad_term = grad_term.reshape(dp_count, tensor_count, CAP, grad_term.shape[1])
    partial_sum = lax.psum_scatter(grad_term, "tensor", scatter_dimension=1, tiled=True)
    own_grad = lax.psum_scatter(partial_sum, "dp", scatter_dimension=0, tiled=True)
    own_grad = own_grad.reshape(CAP, own_grad.shape[3])
    own_grad = own_grad * loss_scale
    own_loss = lax.dynamic_slice_in_dim(slot_loss, device_pos * CAP, CAP, 0)
    slot_pos = jnp.clip(order_pos, 0, CAP - 1)
    hidden_grad = jnp.where(kept_row[:, None], own_grad[slot_pos], 0.0).astype(jnp.bfloat16)
    row_loss = jnp.where(kept_row, own_loss[slot_pos], 0.0)
    return (hidden_grad, row_loss)


def fits(mesh, hidden, out_weight):
    devices = mesh.shape["dp"] * mesh.shape["tensor"]
    return (
        mesh.shape["dp"] % CORES == 0
        and mesh.shape["dp"] > CORES
        and mesh.shape["tensor"] > 1
        and devices <= 32
        and hidden.shape[1] <= 8192
        and hidden.shape[1] % (PIECES * 128) == 0
        and out_weight.shape[0] < 2**24
        and out_weight.shape[0] % (devices * 8) == 0
        and out_weight.shape[0] // devices > TILE
    )


def solution(mesh):
    in_specs = (
        P(("dp", "tensor"), None),
        P(("dp", "tensor"), None),
        P(("dp", "tensor")),
        P(("dp", "tensor")),
        P(("dp", "tensor")),
    )
    out_specs = (P(("dp", "tensor"), None), P(("dp", "tensor")))

    def run(hidden, out_weight, loss_mask, targets, kept_count):
        body = fused_shards if fits(mesh, hidden, out_weight) else shards
        mapped = jax.shard_map(
            body, mesh=mesh, in_specs=in_specs, out_specs=out_specs, check_vma=False
        )
        return mapped(hidden, out_weight, loss_mask, targets, kept_count)

    return run
```
